512 devices in a mesh: tm: 16 (over x_hi, z), space: 32 (over y, x_lo, core).
Axes of the slice: x: 4 (x_hi: 2, x_lo: 2; x = x_hi * 2 + x_lo), y: 8, z: 8, core: 2. Of those that a mesh axis runs over, the one named last changes fastest.
Arguments:
- start_state: float32 [16, 512, 128, 128], P('tm', 'space'), may hold values from -4 to 4
- solid_fraction: float32 [512, 128, 128], P('space'), may hold values from 0 to 0.3
- coarse_gain: float32 [16, 256, 4096], P('tm', 'space'), may hold values from 0.05 to 1
Outputs:
- fine_end: float32 [16, 512, 128, 128], P('tm', 'space')
- coarse_next: float32 [16, 256, 4096], P('tm', 'space')
The draws below stay inside these ranges and needn't reach their ends.
All inputs are finite; a program needn't handle non-finite values.
Results may differ from the reference program's by a relative error of at most 0.0003.
Values sent between devices are 32-bit elements; how exact they have to be, the bound alone decides.
A program may use at most 64 MiB of HBM per device.

```python
import math
import jax
import jax.numpy as jnp
from jax import lax

NX = 128
NY = 128
CZ = 16
STEPS = 4
TIME_SEGMENTS = 16
NZ = 512


def draw_start_state(key, part):
    key = jax.random.fold_in(key, 3)
    full_shape = (TIME_SEGMENTS, NZ, NX, NY)
    return jnp.clip(jax.random.normal(key, full_shape, jnp.float32), -4.0, 4.0)


def draw_solid_fraction(key, part):
    key = jax.random.fold_in(key, 5)
    full_shape = (NZ, NX, NY)
    return jax.random.uniform(key, full_shape, jnp.float32, 0.0, 0.3)


def draw_coarse_gain(key, part):
    key = jax.random.fold_in(key, 7)
    random_subkeys = jax.random.split(key, 7)
    grid_points = (NZ // 2, NX // 2 * (NY // 2))
    keeper = jax.random.bernoulli(random_subkeys[0], 0.5, grid_points)
    quick = jax.random.uniform(random_subkeys[6], (TIME_SEGMENTS,) + grid_points, jnp.float32, 0.05, 0.3)
    growth_rate = jnp.exp(jax.random.uniform(random_subkeys[1], grid_points, jnp.float32, math.log(0.1), math.log(0.4))) / TIME_SEGMENTS
    blocks = jnp.arange(NZ // 2) // (CZ // 2)
    processor_scale = jnp.exp2(jax.random.uniform(random_subkeys[2], (TIME_SEGMENTS, NZ // CZ), jnp.float32, 0.0, 1.3))[:, blocks]
    slice_numbers = jnp.arange(TIME_SEGMENTS)[:, None, None]
    first_pulse = jax.random.randint(random_subkeys[3], grid_points, 0, TIME_SEGMENTS)
    second_pulse = jax.random.randint(random_subkeys[4], grid_points, 0, TIME_SEGMENTS)
    layer_depths = jax.random.uniform(random_subkeys[5], (2,) + grid_points, jnp.float32, 0.55, 0.8)
    pulse_amount = jnp.where(slice_numbers == first_pulse, layer_depths[0], 1.0) * jnp.where(slice_numbers == second_pulse, layer_depths[1], 1.0)
    retained_values = jnp.exp(-growth_rate[None] * processor_scale[:, :, None]) * pulse_amount
    return jnp.where(keeper[None], retained_values, quick).astype(jnp.float32)


def setup_inputs(seed: int = 0) -> dict:
    arg_keys = jax.random.split(jax.random.key(seed), 4)
    return {
        "start_state": draw_start_state(jax.random.fold_in(arg_keys[3], 71), 0),
        "solid_fraction": draw_solid_fraction(jax.random.fold_in(arg_keys[3], 71), 0),
        "coarse_gain": draw_coarse_gain(jax.random.fold_in(arg_keys[3], 71), 0),
    }


time_step = 0.11
solid_drop = 0.9


def diffusivity(solute, solid_part):
    square = solute * solute
    return (1.0 - solid_drop * solid_part) * (1.0 + 0.5 * square / (1.0 + square))


def face_fluxes(solute, spread, direction):
    length = solute.shape[direction]
    solute_low = lax.slice_in_dim(solute, 0, length - 1, axis=direction)
    solute_high = lax.slice_in_dim(solute, 1, length, axis=direction)
    spread_low = lax.slice_in_dim(spread, 0, length - 1, axis=direction)
    spread_high = lax.slice_in_dim(spread, 1, length, axis=direction)
    return 0.5 * (spread_low + spread_high) * (solute_high - solute_low)


def side_change(fluxes, direction):
    plane_shape = list(fluxes.shape)
    plane_shape[direction] = 1
    border = jnp.zeros(plane_shape, fluxes.dtype)
    return jnp.concatenate([fluxes, border], direction) - jnp.concatenate([border, fluxes], direction)


def fine_step(solute, solid_part):
    spread = diffusivity(solute, solid_part)
    change = side_change(face_fluxes(solute, spread, 0), 0)
    change = change + side_change(face_fluxes(solute, spread, 1), 1)
    change = change + side_change(face_fluxes(solute, spread, 2), 2)
    return solute + time_step * change


def restrict(volume):
    paired = volume.reshape(volume.shape[0] // 2, 2, volume.shape[1] // 2, 2, volume.shape[2]).sum(axis=(1, 3))
    paired = paired[:, :, 0::2] + paired[:, :, 1::2]
    return (0.125 * paired).reshape(paired.shape[0], -1)


def reference(start_state, solid_fraction, coarse_gain):
    def one_slice(initial):
        solute = initial
        for _ in range(STEPS):
            solute = fine_step(solute, solid_fraction)
        return solute, restrict(solute), restrict(initial)

    fine_end, coarse_fine, coarse_start = lax.map(one_slice, start_state)

    def sweep(previous, inputs):
        coarse_end, coarse_begin, amplify, number = inputs
        updated = jnp.where(number == 0, coarse_end, amplify * previous + (coarse_end - amplify * coarse_begin))
        return updated, updated

    slice_numbers = jnp.arange(TIME_SEGMENTS, dtype=jnp.int32)
    empty_start = jnp.zeros(coarse_fine.shape[1:], jnp.float32)
    final_state, coarse_next = lax.scan(sweep, empty_start, (coarse_fine, coarse_start, coarse_gain, slice_numbers))
    return fine_end, coarse_next
```

```python
import functools

import jax
import jax.numpy as jnp
from jax import lax
from jax.experimental import pallas as pl
from jax.experimental.pallas import tpu as pltpu
from jax.sharding import PartitionSpec as P

STEPS = 4
H = STEPS
F32 = jnp.float32
MESH = pl.DeviceIdType.MESH

time_step = 0.11
solid_drop = 0.9

ROWS = 32
NP = 2


def kernel(
    nt, ns, c_hbm, s_hbm, g_hbm, fine_ref, coarse_ref,
    c0, c1, c2, c3, c4, d0, d1, d2, d3, bb, fz, fx, vs, ly,
    gv, gl, rs, jl, gb, jb, xb, ob,
    ld_sem, halo_send, halo_recv, g_send, g_recv, j_send, j_recv, x_send, x_recv, out_sem,
):
    planes, nx, ny = c_hbm.shape
    cs = (c0, c1, c2, c3, c4)
    ds = (d0, d1, d2, d3)
    t = lax.axis_index("tm")
    s = lax.axis_index("space")
    core = lax.rem(s, 2)
    step = 2 * core - 1
    first = jnp.where(core == 1, 0, planes + 2 * H - 1)

    def at(q):
        return first + step * q

    barrier = pltpu.get_barrier_semaphore()
    for k in range(1, nt):
        pl.semaphore_signal(barrier, inc=1, device_id={"tm": lax.rem(t + k, nt)}, device_id_type=MESH)
    fast = s + 1 - 2 * core
    slow = s - 1 + 2 * core
    inner = jnp.logical_and(slow >= 0, slow < ns)
    pl.semaphore_signal(barrier, inc=1, device_id={"space": fast}, device_id_type=MESH)

    @pl.when(inner)
    def _():
        pl.semaphore_signal(barrier, inc=1, device_id={"space": slow}, device_id_type=MESH)

    loads = [
        pltpu.make_async_copy(c_hbm, c0.at[pl.ds(H, planes), pl.ds(0, nx)], ld_sem.at[0]),
        pltpu.make_async_copy(s_hbm, bb.at[pl.ds(H, planes)], ld_sem.at[1]),
        pltpu.make_async_copy(g_hbm, gv, ld_sem.at[2]),
    ]
    for cp in loads:
        cp.start()

    row = lax.broadcasted_iota(jnp.int32, (2 * ny, ny), 0)
    lane = lax.broadcasted_iota(jnp.int32, (2 * ny, ny), 1)
    ly[...] = jnp.where(row // 2 == lane, F32(0.125), F32(0.0))
    for l in range(STEPS):
        fx[l, pl.ds(0, 8), :] = jnp.zeros((8, ny), F32)

    def restrict(ref, lo, hi):
        vs[...] = ref[lo, pl.ds(0, nx), :] + ref[hi, pl.ds(0, nx), :]
        parts = []
        for gg in range(2):
            halves = []
            for h in range(2):
                base = 4 * gg + 2 * h
                halves.append(
                    vs[pl.ds(base, nt, stride=8), :] + vs[pl.ds(base + 1, nt, stride=8), :]
                )
            parts.append(jnp.concatenate(halves, axis=1))
        both = jnp.concatenate(parts, axis=0)
        out = jnp.dot(both, ly[...], precision=lax.Precision.HIGHEST, preferred_element_type=F32)
        return out[:nt], out[nt:]

    per = planes // 2 // NP
    rows = 2 * per

    loads[2].wait()
    for g in range(gv.shape[1] // 128):
        v = gv[:, pl.ds(g * 128, 128)]
        for piece in range(NP):
            gl[g // 2, piece, pl.ds(g % 2, per, stride=2), :] = v[piece * per : (piece + 1) * per]

    loads[0].wait()

    @pl.loop(0, planes // 2)
    def _(p):
        piece = p // per
        i = lax.rem(p, per)
        for gg, part in enumerate(restrict(c0, H + 2 * p, H + 2 * p + 1)):
            rs[piece, pl.ds(2 * i + gg, nt, stride=rows), :] = part

    gb[t] = gl[t]
    loads[1].wait()
    pl.semaphore_wait(barrier, jnp.where(inner, nt + 1, nt))

    def sends(to_high, dev, kind, n):
        out = []
        for j in range(H // n):
            src = jnp.where(to_high, planes - n * (j + 1), n * j)
            dst = jnp.where(to_high, H - n * (j + 1), H + planes + n * j)
            for a, (ref, buf) in enumerate(((c_hbm, c0), (s_hbm, bb))):
                to = buf.at[pl.ds(dst, n), pl.ds(0, nx)]
                out.append(
                    pltpu.make_async_remote_copy(
                        src_ref=ref.at[pl.ds(src, n)], dst_ref=to,
                        send_sem=halo_send.at[kind, a, j], recv_sem=halo_recv.at[kind, a, j],
                        device_id={"space": dev}, device_id_type=MESH,
                    )
                )
        return out

    fast_copies = sends(core == 0, fast, 0, H)
    slow_copies = sends(core == 1, slow, 1, 1)
    for cp in fast_copies:
        cp.start()

    @pl.when(inner)
    def _():
        for cp in slow_copies:
            cp.start()

    def mirrors():
        out = []
        for j in range(H):
            src = jnp.where(core == 1, planes - 1 - j, j)
            dst = jnp.where(core == 1, H + planes + j, H - 1 - j)
            for a, (ref, buf) in enumerate(((c_hbm, c0), (s_hbm, bb))):
                out.append(
                    pltpu.make_async_copy(ref.at[src], buf.at[dst, pl.ds(0, nx)], halo_recv.at[1, a, j])
                )
        return out

    @pl.when(jnp.logical_not(inner))
    def _():
        for cp in mirrors():
            cp.start()

    def to_all(src, dst, send, recv):
        for k in range(1, nt):
            q = lax.rem(t + k, nt)
            pltpu.make_async_remote_copy(
                src_ref=src(q), dst_ref=dst, send_sem=send, recv_sem=recv,
                device_id={"tm": q}, device_id_type=MESH,
            ).start()

    def wait_all(ref, sem):
        part = ref.at[pl.ds(0, nt - 1)]
        pltpu.make_async_copy(part, part, sem).wait()

    to_all(lambda q: gl.at[q], gb.at[t], g_send, g_recv)

    def wait_halo(kind, j, n):
        for a, buf in enumerate((c0, bb)):
            part = buf.at[pl.ds(0, n), pl.ds(0, nx)]
            pltpu.make_async_copy(part, part, halo_recv.at[kind, a, j]).wait()

    wait_halo(0, 0, H)

    def spread(c, b):
        return b * (3.0 - 1.0 / (1.0 + c * c))

    def prepare(q):
        p = at(q)
        for r in range(0, nx, ROWS):
            w = pl.ds(r, ROWS)
            b = F32(time_step * 0.25) - F32(time_step * 0.25 * solid_drop) * bb[p, w, :]
            bb[p, w, :] = b
            d0[p, w, :] = spread(c0[p, w, :], b)

    def start_level(l):
        p, b = at(l), at(l - 1)
        c, d = cs[l - 1], ds[l - 1]
        for r in range(0, nx, ROWS):
            w = pl.ds(r, ROWS)
            fz[l - 1, w, :] = (d[b, w, :] + d[p, w, :]) * (c[p, w, :] - c[b, w, :])

    lanes = lax.broadcasted_iota(jnp.int32, (ROWS, ny), 1)
    inside_y = jnp.where(lanes < ny - 1, F32(1.0), F32(0.0))
    rows_in = lax.broadcasted_iota(jnp.int32, (ROWS, ny), 0)
    inside_x = rows_in < ROWS - 1

    def advance(l, q):
        p, a = at(q), at(q + 1)
        c, d = cs[l - 1], ds[l - 1]
        for r in range(0, nx, ROWS):
            w = pl.ds(r, ROWS)
            up = pl.ds(r + 1, ROWS)
            here = c[p, w, :]
            dh = d[p, w, :]
            ahead = (dh + d[a, w, :]) * (c[a, w, :] - here)
            change = ahead - fz[l - 1, w, :]
            fz[l - 1, w, :] = ahead
            flux = (dh + d[p, up, :]) * (c[p, up, :] - here)
            if r + ROWS == nx:
                flux = jnp.where(inside_x, flux, F32(0.0))
            fx[l - 1, pl.ds(r + 8, ROWS), :] = flux
            change = change + (flux - fx[l - 1, pl.ds(r + 7, ROWS), :])
            side = (dh + pltpu.roll(dh, ny - 1, 1)) * (pltpu.roll(here, ny - 1, 1) - here)
            side = side * inside_y
            change = change + (side - pltpu.roll(side, 1, 1))
            new = here + change
            cs[l][p, w, :] = new
            if l < STEPS:
                ds[l][p, w, :] = spread(new, bb[p, w, :])

    def front(k, levels):
        prepare(k + 1)
        for l in range(1, levels + 1):
            advance(l, k - (l - 1))

    prepare(0)
    prepare(1)
    for l in range(1, STEPS):
        start_level(l)
        for k in (2 * l - 1, 2 * l):
            front(k, l)
    start_level(STEPS)

    def body(m):
        @pl.when(m >= planes // 2 - H // 2)
        def _():
            j = 2 * m - (planes - H)
            wait_halo(1, j, 1)
            wait_halo(1, j + 1, 1)

        for k in range(2):
            front(2 * STEPS - 1 + 2 * m + k, STEPS)
        q = H + 2 * m
        lo = jnp.minimum(at(q), at(q + 1))
        pltpu.make_async_copy(
            c4.at[pl.ds(lo, 2)], fine_ref.at[pl.ds(lo - H, 2)], out_sem.at[0]
        ).start()
        plane = (lo - H) // 2
        piece = plane // per
        i = lax.rem(plane, per)
        for gg, part in enumerate(restrict(c4, lo, lo + 1)):
            jl[piece, pl.ds(2 * i + gg, nt, stride=rows), :] = part

    later = jnp.where(t == 0, F32(0.0), F32(1.0))
    order = [jnp.where(core == 1, n, NP - 1 - n) for n in range(NP)]

    for n in range(NP):
        pl.loop(n * per, (n + 1) * per)(body)
        piece = order[n]

        @pl.loop(0, nt)
        def _(o):
            w = pl.ds(pl.multiple_of(o * rows, rows), rows)
            jl[piece, w, :] = jl[piece, w, :] - later * gl[o, piece] * rs[piece, w, :]

        def own(q):
            return pl.ds(pl.multiple_of(q * rows, rows), rows)

        to_all(lambda q: jl.at[piece, own(q)], jb.at[piece, t], j_send.at[n], j_recv.at[n])
        jb[piece, t] = jl[piece, own(t), :]

    wait_all(gb, g_recv)
    for n in range(NP):
        piece = order[n]
        wait_all(jb.at[piece], j_recv.at[n])
        x = jb[piece, 0]
        xb[piece, 0] = x
        for m in range(1, nt):
            x = gb[m, piece] * x + jb[piece, m]
            xb[piece, m] = x
        to_all(lambda q: xb.at[piece, q], ob.at[piece, t], x_send.at[n], x_recv.at[n])
        ob[piece, t] = xb[piece, t]

    for n in range(NP):
        wait_all(ob.at[order[n]], x_recv.at[n])
    for g in range(gv.shape[1] // 128):
        for piece in range(NP):
            coarse_ref[pl.ds(piece * per, per), pl.ds(g * 128, 128)] = ob[
                piece, g // 2, pl.ds(g % 2, per, stride=2), :
            ]

    for cp in fast_copies:
        cp.wait_send()

    @pl.when(inner)
    def _():
        for cp in slow_copies:
            cp.wait_send()

    wait_all(gb, g_send)
    for n in range(NP):
        wait_all(jb.at[0], j_send.at[n])
        wait_all(xb.at[0], x_send.at[n])
    pltpu.make_async_copy(c4.at[pl.ds(0, planes)], fine_ref, out_sem.at[0]).wait()


def on_device(nt, ns, start_state, solid_fraction, coarse_gain):
    planes, nx, ny = solid_fraction.shape
    ext = planes + 2 * H
    cp, cells = coarse_gain.shape[1:]
    rows = cp * cells // 128 // nt // NP
    vmem = lambda *shape: pltpu.VMEM(shape, F32)
    dma = pltpu.SemaphoreType.DMA
    fine, coarse = pl.pallas_call(
        functools.partial(kernel, nt, ns),
        name="parareal",
        out_shape=(
            pltpu.VMEM((planes, nx, ny), F32),
            pltpu.VMEM((cp, cells), F32),
        ),
        in_specs=[pl.BlockSpec(memory_space=pltpu.HBM)] * 3,
        out_specs=(pl.BlockSpec(memory_space=pltpu.VMEM), pl.BlockSpec(memory_space=pltpu.VMEM)),
        scratch_shapes=[
            *[vmem(ext, nx + 8, ny)] * 4, vmem(ext, nx, ny),
            *[vmem(ext, nx + 8, ny)] * 4, vmem(ext, nx, ny),
            vmem(STEPS, nx, ny), vmem(STEPS, nx + 8, ny), vmem(nx, ny), vmem(2 * ny, ny),
            vmem(cp, cells), vmem(nt, NP, rows, 128), vmem(NP, nt * rows, 128), vmem(NP, nt * rows, 128),
            vmem(nt, NP, rows, 128), vmem(NP, nt, rows, 128), vmem(NP, nt, rows, 128), vmem(NP, nt, rows, 128),
            dma((3,)), dma((2, 2, H)), dma((2, 2, H)), dma, dma,
            dma((NP,)), dma((NP,)), dma((NP,)), dma((NP,)), dma((1,)),
        ],
        compiler_params=pltpu.CompilerParams(
            collective_id=0, has_side_effects=True, vmem_limit_bytes=46 * 2**20
        ),
    )(*[pltpu.with_memory_space_constraint(v, pltpu.HBM) for v in (start_state[0], solid_fraction, coarse_gain[0])])
    return fine[None], coarse[None]


def solution(mesh):
    nt, ns = mesh.shape["tm"], mesh.shape["space"]
    placed = (P("tm", "space", None, None), P("space", None, None), P("tm", "space", None))
    return jax.shard_map(
        functools.partial(on_device, nt, ns),
        mesh=mesh,
        in_specs=placed,
        out_specs=(P("tm", "space", None, None), P("tm", "space", None)),
        check_vma=False,
    )
```

```python
import functools

import jax
import jax.numpy as jnp
from jax import lax
from jax.experimental import pallas as pl
from jax.experimental.pallas import tpu as pltpu
from jax.sharding import PartitionSpec as P

STEPS = 4
H = STEPS
F32 = jnp.float32
MESH = pl.DeviceIdType.MESH

time_step = 0.11
solid_drop = 0.9

ROWS = 32
NP = 4
EARLY = 4
GROUP = 4


def kernel(
    nt, ns, c_hbm, s_hbm, g_hbm, fine_ref, coarse_ref,
    c0, solid, c1, c2, c3, d0, d1, d2, d3, c_next, d_next, inflow, outflow, fz, vs, ly,
    gv, gl, rs, jl, gb, jb, xb, ob,
    ld_sem, halo_send, halo_recv, g_send, g_recv, j_send, j_recv, x_send, x_recv,
):
    planes, nx, ny = c_hbm.shape
    cs = (c0, c1, c2, c3)
    ds = (d0, d1, d2, d3)
    half = nt // 2
    no = 2 * EARLY
    t = lax.axis_index("tm")
    s = lax.axis_index("space")
    core = lax.rem(s, 2)
    step = 2 * core - 1
    first = jnp.where(core == 1, 0, planes + 2 * H - 1)

    def at(q):
        return first + step * q

    owners = [(o // EARLY) * half + o % EARLY for o in range(no)]
    owner = lax.rem(t, half) < EARLY
    mine = (t // half) * EARLY + lax.rem(t, half)
    group = t // GROUP

    barrier = pltpu.get_barrier_semaphore()

    @pl.when(owner)
    def _():
        for k in range(1, nt):
            pl.semaphore_signal(barrier, inc=1, device_id={"tm": lax.rem(t + k, nt)}, device_id_type=MESH)

    fast = s + 1 - 2 * core
    slow = s - 1 + 2 * core
    inner = jnp.logical_and(slow >= 0, slow < ns)
    pl.semaphore_signal(barrier, inc=1, device_id={"space": fast}, device_id_type=MESH)

    other = lax.rem(t + half, nt)

    @pl.when(inner)
    def _():
        for to in (t, other):
            pl.semaphore_signal(barrier, inc=1, device_id={"tm": to, "space": slow}, device_id_type=MESH)

    loads = [
        pltpu.make_async_copy(c_hbm, c0.at[pl.ds(H, planes)], ld_sem.at[0]),
        pltpu.make_async_copy(s_hbm, solid.at[pl.ds(H, planes)], ld_sem.at[1]),
        pltpu.make_async_copy(g_hbm, gv, ld_sem.at[2]),
    ]
    for cp in loads:
        cp.start()

    def sends(to_high, dev, kind, n, solid_to):
        out = []
        for j in range(H // n):
            src = jnp.where(to_high, planes - n * (j + 1), n * j)
            dst = jnp.where(to_high, H - n * (j + 1), H + planes + n * j)
            for a, (ref, buf) in enumerate(((c_hbm, c0), (s_hbm, solid))):
                to = buf.at[pl.ds(dst, n)]
                out.append(
                    pltpu.make_async_remote_copy(
                        src_ref=ref.at[pl.ds(src, n)], dst_ref=to,
                        send_sem=halo_send.at[kind, a, j], recv_sem=halo_recv.at[kind, a, j],
                        device_id={"tm": (t, solid_to)[a], "space": dev}, device_id_type=MESH,
                    )
                )
        return out

    fast_copies = sends(core == 0, fast, 0, H, t)
    slow_copies = sends(core == 1, slow, 1, 1, other)

    def mirrors():
        out = []
        for j in range(H):
            src = jnp.where(core == 1, planes - 1 - j, j)
            dst = jnp.where(core == 1, H + planes + j, H - 1 - j)
            for a, (ref, buf) in enumerate(((c_hbm, c0), (s_hbm, solid))):
                out.append(
                    pltpu.make_async_copy(ref.at[src], buf.at[dst], halo_recv.at[1, a, j])
                )
        return out

    peers = jnp.where(owner, no, no + 1) + jnp.where(inner, 2, 0)
    pl.semaphore_wait(barrier, peers)

    @pl.when(inner)
    def _():
        for cp in slow_copies:
            cp.start()

    @pl.when(jnp.logical_not(inner))
    def _():
        for cp in mirrors():
            cp.start()

    for cp in fast_copies:
        cp.start()

    row = lax.broadcasted_iota(jnp.int32, (2 * ny, ny), 0)
    lane = lax.broadcasted_iota(jnp.int32, (2 * ny, ny), 1)
    ly[...] = jnp.where(row // 2 == lane, F32(0.125), F32(0.0))

    per = planes // 2 // NP
    groups = 32 // no
    rows = groups * per

    def restrict(ref, lo, hi):
        vs[...] = ref[lo] + ref[hi]
        parts = []
        for gg in range(groups):
            halves = []
            for h in range(2):
                base = 4 * gg + 2 * h
                halves.append(
                    vs[pl.ds(base, no, stride=nx // no), :] + vs[pl.ds(base + 1, no, stride=nx // no), :]
                )
            parts.append(jnp.concatenate(halves, axis=1))
        both = jnp.concatenate(parts, axis=0)
        out = jnp.dot(both, ly[...], precision=lax.Precision.HIGHEST, preferred_element_type=F32)
        return [out[no * gg : no * (gg + 1)] for gg in range(groups)]

    loads[2].wait()
    for g in range(gv.shape[1] // 128):
        v = gv[:, pl.ds(g * 128, 128)]
        for piece in range(NP):
            gl[g // groups, piece, pl.ds(g % groups, per, stride=groups), :] = v[
                piece * per : (piece + 1) * per
            ]

    def to_owners(src, dst, send, recv):
        for o in range(no):
            @pl.when(t != owners[o])
            def _(o=o):
                pltpu.make_async_remote_copy(
                    src_ref=src(o), dst_ref=dst, send_sem=send, recv_sem=recv,
                    device_id={"tm": owners[o]}, device_id_type=MESH,
                ).start()

    def wait_blocks(ref, n, sem):
        part = ref.at[pl.ds(0, n)]
        pltpu.make_async_copy(part, part, sem).wait()

    def wait_either(cond, ref, n, sem):
        @pl.when(cond)
        def _():
            wait_blocks(ref, n - 1, sem)

        @pl.when(jnp.logical_not(cond))
        def _():
            wait_blocks(ref, n, sem)

    to_owners(lambda o: gl.at[o], gb.at[t], g_send, g_recv.at[group])

    @pl.when(owner)
    def _():
        gb[t] = gl[mine]

    loads[0].wait()

    @pl.loop(0, planes // 2)
    def _(p):
        piece = p // per
        i = lax.rem(p, per)
        for gg, part in enumerate(restrict(c0, H + 2 * p, H + 2 * p + 1)):
            rs[piece, pl.ds(groups * i + gg, no, stride=rows), :] = part

    loads[1].wait()

    def wait_halo(kind, j, n):
        for a, buf in enumerate((c0, solid)):
            part = buf.at[pl.ds(0, n)]
            pltpu.make_async_copy(part, part, halo_recv.at[kind, a, j]).wait()

    wait_halo(0, 0, H)

    def spread(c, q, w):
        b = F32(time_step * 0.25) - F32(time_step * 0.25 * solid_drop) * solid[at(q[0] + q[1]), w, :]
        return b * (3.0 - 1.0 / (1.0 + c * c))

    def state(l, q, w):
        return cs[l][q[1] % 2, w, :] if l else c0[at(q[0] + q[1]), w, :]

    def diff(l, q, w):
        return ds[l][q[1] % 2, w, :]

    def after(q, n):
        return (q[0], q[1] + n)

    def store(l, q, w, c):
        i = q[1] % 2
        d = spread(c, q, w)
        if l:
            cs[l][i, w, :] = c
        ds[l][i, w, :] = d
        c_next[l, i, w, :] = pltpu.roll(c, ny - 1, 1)
        d_next[l, i, w, :] = pltpu.roll(d, ny - 1, 1)

    chunks = [pl.ds(r, ROWS) for r in range(0, nx, ROWS)]

    def prepare(q):
        for w in chunks:
            store(0, q, w, c0[at(q[0] + q[1]), w, :])

    def start_level(l):
        q, b = (0, l), (0, l - 1)
        for w in chunks:
            fz[l - 1, w, :] = (diff(l - 1, b, w) + diff(l - 1, q, w)) * (
                state(l - 1, q, w) - state(l - 1, b, w)
            )

    def advance(l, q):
        i = q[1] % 2
        for w in chunks:
            here, dh = state(l - 1, q, w), diff(l - 1, q, w)
            ahead = (dh + diff(l - 1, after(q, 1), w)) * (state(l - 1, after(q, 1), w) - here)
            new = (here + inflow[l - 1, i, w, :]) + (
                (ahead - fz[l - 1, w, :]) - outflow[l - 1, i, w, :]
            )
            fz[l - 1, w, :] = ahead
            if l < STEPS:
                store(l, q, w, new)
            else:
                fine_ref[at(q[0] + q[1]) - H, w, :] = new

    lanes = lax.broadcasted_iota(jnp.int32, (nx, ny), 1)
    rows_in = lax.broadcasted_iota(jnp.int32, (nx, ny), 0)

    def in_plane(l, q):
        i, w = q[1] % 2, pl.ds(0, nx)
        here, dh = state(l, q, w), diff(l, q, w)
        side = (dh + d_next[l, i]) * (c_next[l, i] - here)
        side = jnp.where(lanes < ny - 1, side, F32(0.0))
        outflow[l, i] = pltpu.roll(side, 1, 1)
        flux = (dh + pltpu.roll(dh, nx - 1, 0)) * (pltpu.roll(here, nx - 1, 0) - here)
        flux = jnp.where(rows_in < nx - 1, flux, F32(0.0))
        inflow[l, i] = (flux - pltpu.roll(flux, 1, 0)) + side

    def front(k, levels):
        prepare(after(k, 1))
        for l in range(1, levels + 1):
            advance(l, after(k, 1 - l))
        in_plane(0, after(k, 1))
        for l in range(1, min(levels, STEPS - 1) + 1):
            in_plane(l, after(k, 1 - l))

    prepare((0, 0))
    prepare((0, 1))
    in_plane(0, (0, 1))
    for l in range(1, STEPS):
        start_level(l)
        for k in (2 * l - 1, 2 * l):
            front((0, k), l)
    start_level(STEPS)

    def body(m):
        @pl.when(m >= planes // 2 - H // 2)
        def _():
            j = 2 * m - (planes - H)
            wait_halo(1, j, 1)
            wait_halo(1, j + 1, 1)

        for k in range(2):
            front((2 * m, 2 * STEPS - 1 + k), STEPS)
        q = H + 2 * m
        lo = jnp.minimum(at(q), at(q + 1)) - H
        plane = lo // 2
        piece = plane // per
        i = lax.rem(plane, per)
        for gg, part in enumerate(restrict(fine_ref, lo, lo + 1)):
            jl[piece, pl.ds(groups * i + gg, no, stride=rows), :] = part

    later = jnp.where(t == 0, F32(0.0), F32(1.0))

    def own(o):
        return pl.ds(pl.multiple_of(o * rows, rows), rows)

    @pl.loop(0, NP)
    def _(n):
        pl.loop(n * per, (n + 1) * per)(body)
        piece = jnp.where(core == 1, n, NP - 1 - n)
        for o in range(no):
            w = own(o)
            jl[piece, w, :] = jl[piece, w, :] - later * gl[o, piece] * rs[piece, w, :]
        to_owners(lambda o: jl.at[piece, own(o)], jb.at[piece, t], j_send.at[n], j_recv.at[n, group])

        @pl.when(owner)
        def _():
            jb[piece, t] = jl[piece, own(mine), :]

    def scan(n, gr):
        piece = jnp.where(core == 1, n, NP - 1 - n)
        wait_either(group == gr, jb.at[piece], GROUP, j_recv.at[n, gr])
        for m in range(gr * GROUP, (gr + 1) * GROUP):
            x = jb[piece, m]
            if m:
                x = gb[m, piece] * xb[piece, m - 1] + x
            xb[piece, m] = x
        for m in range(gr * GROUP, (gr + 1) * GROUP):
            @pl.when(t == m)
            def _(m=m):
                ob[piece, mine] = xb[piece, m]

            @pl.when(t != m)
            def _(m=m):
                pltpu.make_async_remote_copy(
                    src_ref=xb.at[piece, m], dst_ref=ob.at[piece, mine],
                    send_sem=x_send.at[n], recv_sem=x_recv.at[n],
                    device_id={"tm": m}, device_id_type=MESH,
                ).start()

    @pl.when(owner)
    def _():
        for grs in ((0,), (1, 2), (3,)):
            for gr in grs:
                wait_either(group == gr, gb, GROUP, g_recv.at[gr])

            @pl.loop(0, NP)
            def _(n):
                for gr in grs:
                    scan(n, gr)

    for n in range(NP):
        wait_either(owner, ob.at[0], no, x_recv.at[n])
    for g in range(gv.shape[1] // 128):
        for piece in range(NP):
            coarse_ref[pl.ds(piece * per, per), pl.ds(g * 128, 128)] = ob[
                piece, g // groups, pl.ds(g % groups, per, stride=groups), :
            ]

    for cp in fast_copies:
        cp.wait_send()

    @pl.when(inner)
    def _():
        for cp in slow_copies:
            cp.wait_send()

    wait_either(owner, gl, no, g_send)
    for n in range(NP):
        wait_either(owner, ob.at[0], no, j_send.at[n])

        @pl.when(owner)
        def _(n=n):
            wait_blocks(xb.at[0], nt - 1, x_send.at[n])


def on_device(nt, ns, start_state, solid_fraction, coarse_gain):
    planes, nx, ny = solid_fraction.shape
    ext = planes + 2 * H
    cp, cells = coarse_gain.shape[1:]
    no = 2 * EARLY
    rows = cp * cells // 128 // no // NP
    vmem = lambda *shape: pltpu.VMEM(shape, F32)
    dma = pltpu.SemaphoreType.DMA
    fine, coarse = pl.pallas_call(
        functools.partial(kernel, nt, ns),
        name="parareal",
        out_shape=(
            pltpu.VMEM((planes, nx, ny), F32),
            pltpu.VMEM((cp, cells), F32),
        ),
        in_specs=[pl.BlockSpec(memory_space=pltpu.HBM)] * 3,
        out_specs=(pl.BlockSpec(memory_space=pltpu.VMEM), pl.BlockSpec(memory_space=pltpu.VMEM)),
        scratch_shapes=[
            *[vmem(ext, nx, ny)] * 2, *[vmem(2, nx, ny)] * 7, *[vmem(STEPS, 2, nx, ny)] * 4,
            vmem(STEPS, nx, ny), vmem(nx, ny), vmem(2 * ny, ny),
            vmem(cp, cells), vmem(no, NP, rows, 128), vmem(NP, no * rows, 128), vmem(NP, no * rows, 128),
            vmem(nt, NP, rows, 128), vmem(NP, nt, rows, 128), vmem(NP, nt, rows, 128), vmem(NP, no, rows, 128),
            dma((3,)), dma((2, 2, H)), dma((2, 2, H)), dma, dma((nt // GROUP,)),
            dma((NP,)), dma((NP, nt // GROUP)), dma((NP,)), dma((NP,)),
        ],
        compiler_params=pltpu.CompilerParams(
            collective_id=0, has_side_effects=True, vmem_limit_bytes=46 * 2**20
        ),
    )(*[pltpu.with_memory_space_constraint(v, pltpu.HBM) for v in (start_state[0], solid_fraction, coarse_gain[0])])
    return fine[None], coarse[None]


def solution(mesh):
    nt, ns = mesh.shape["tm"], mesh.shape["space"]
    placed = (P("tm", "space", None, None), P("space", None, None), P("tm", "space", None))
    return jax.shard_map(
        functools.partial(on_device, nt, ns),
        mesh=mesh,
        in_specs=placed,
        out_specs=(P("tm", "space", None, None), P("tm", "space", None)),
        check_vma=False,
    )
```

```python
import functools

import jax
import jax.numpy as jnp
from jax import lax
from jax.experimental import pallas as pl
from jax.experimental.pallas import tpu as pltpu
from jax.sharding import PartitionSpec as P

STEPS = 4
H = STEPS
F32 = jnp.float32
MESH = pl.DeviceIdType.MESH

time_step = 0.11
solid_drop = 0.9

ROWS = 32
NP = 4
GROUP = 4


def kernel(
    nt, ns, c_hbm, s_hbm, g_hbm, fine_ref, coarse_ref,
    c0, solid, c1, c2, c3, d0, d1, d2, d3, c_next, d_next, inflow, outflow, fz, vs, ly,
    gv, gl, rs, jl, gb, jb, xb, ob,
    ld_sem, halo_send, halo_recv, g_send, g_recv, j_send, j_recv, x_send, x_recv, ready,
):
    planes, nx, ny = c_hbm.shape
    cs = (c0, c1, c2, c3)
    ds = (d0, d1, d2, d3)
    half = nt // 2
    no = nt
    t = lax.axis_index("tm")
    s = lax.axis_index("space")
    core = lax.rem(s, 2)
    step = 2 * core - 1
    first = jnp.where(core == 1, 0, planes + 2 * H - 1)

    def at(q):
        return first + step * q

    place = lax.rem(t, half)
    group = t // GROUP
    partners = [lax.rem(t + k, nt) for k in range(1, nt)]

    barrier = pltpu.get_barrier_semaphore()
    for q in partners:
        @pl.when(lax.rem(q, half) >= place)
        def _(q=q):
            pl.semaphore_signal(barrier, inc=1, device_id={"tm": q}, device_id_type=MESH)

    fast = s + 1 - 2 * core
    slow = s - 1 + 2 * core
    inner = jnp.logical_and(slow >= 0, slow < ns)
    pl.semaphore_signal(barrier, inc=1, device_id={"space": fast}, device_id_type=MESH)

    other = lax.rem(t + half, nt)

    @pl.when(inner)
    def _():
        for to in (t, other):
            pl.semaphore_signal(barrier, inc=1, device_id={"tm": to, "space": slow}, device_id_type=MESH)

    loads = [
        pltpu.make_async_copy(c_hbm, c0.at[pl.ds(H, planes)], ld_sem.at[0]),
        pltpu.make_async_copy(s_hbm, solid.at[pl.ds(H, planes)], ld_sem.at[1]),
        pltpu.make_async_copy(g_hbm, gv, ld_sem.at[2]),
    ]
    for cp in loads:
        cp.start()

    def sends(to_high, dev, kind, n, solid_to):
        out = []
        for j in range(H // n):
            src = jnp.where(to_high, planes - n * (j + 1), n * j)
            dst = jnp.where(to_high, H - n * (j + 1), H + planes + n * j)
            for a, (ref, buf) in enumerate(((c_hbm, c0), (s_hbm, solid))):
                to = buf.at[pl.ds(dst, n)]
                out.append(
                    pltpu.make_async_remote_copy(
                        src_ref=ref.at[pl.ds(src, n)], dst_ref=to,
                        send_sem=halo_send.at[kind, a, j], recv_sem=halo_recv.at[kind, a, j],
                        device_id={"tm": (t, solid_to)[a], "space": dev}, device_id_type=MESH,
                    )
                )
        return out

    fast_copies = sends(core == 0, fast, 0, H, t)
    slow_copies = sends(core == 1, slow, 1, 1, other)

    def mirrors():
        out = []
        for j in range(H):
            src = jnp.where(core == 1, planes - 1 - j, j)
            dst = jnp.where(core == 1, H + planes + j, H - 1 - j)
            for a, (ref, buf) in enumerate(((c_hbm, c0), (s_hbm, solid))):
                out.append(
                    pltpu.make_async_copy(ref.at[src], buf.at[dst], halo_recv.at[1, a, j])
                )
        return out

    pl.semaphore_wait(barrier, 2 * place + 2 + jnp.where(inner, 2, 0))

    @pl.when(inner)
    def _():
        for cp in slow_copies:
            cp.start()

    @pl.when(jnp.logical_not(inner))
    def _():
        for cp in mirrors():
            cp.start()

    for cp in fast_copies:
        cp.start()

    for q in partners:
        @pl.when(lax.rem(q, half) < place)
        def _(q=q):
            pl.semaphore_signal(ready, inc=1, device_id={"tm": q}, device_id_type=MESH)

    row = lax.broadcasted_iota(jnp.int32, (2 * ny, ny), 0)
    lane = lax.broadcasted_iota(jnp.int32, (2 * ny, ny), 1)
    ly[...] = jnp.where(row // 2 == lane, F32(0.125), F32(0.0))

    per = planes // 2 // NP
    groups = 32 // no
    rows = groups * per

    def restrict(ref, lo, hi):
        vs[...] = ref[lo] + ref[hi]
        parts = []
        for gg in range(groups):
            halves = []
            for h in range(2):
                base = 4 * gg + 2 * h
                halves.append(
                    vs[pl.ds(base, no, stride=nx // no), :] + vs[pl.ds(base + 1, no, stride=nx // no), :]
                )
            parts.append(jnp.concatenate(halves, axis=1))
        both = jnp.concatenate(parts, axis=0)
        out = jnp.dot(both, ly[...], precision=lax.Precision.HIGHEST, preferred_element_type=F32)
        return [out[no * gg : no * (gg + 1)] for gg in range(groups)]

    loads[2].wait()
    for g in range(gv.shape[1] // 128):
        v = gv[:, pl.ds(g * 128, 128)]
        for piece in range(NP):
            gl[g // groups, piece, pl.ds(g % groups, per, stride=groups), :] = v[
                piece * per : (piece + 1) * per
            ]

    def to_owners(src, dst, send, recv):
        for q in partners:
            pltpu.make_async_remote_copy(
                src_ref=src(q), dst_ref=dst, send_sem=send, recv_sem=recv,
                device_id={"tm": q}, device_id_type=MESH,
            ).start()

    def wait_blocks(ref, n, sem):
        part = ref.at[pl.ds(0, n)]
        pltpu.make_async_copy(part, part, sem).wait()

    def wait_either(cond, ref, n, sem):
        @pl.when(cond)
        def _():
            wait_blocks(ref, n - 1, sem)

        @pl.when(jnp.logical_not(cond))
        def _():
            wait_blocks(ref, n, sem)

    gb[t] = gl[t]

    loads[0].wait()

    @pl.loop(0, planes // 2)
    def _(p):
        piece = p // per
        i = lax.rem(p, per)
        for gg, part in enumerate(restrict(c0, H + 2 * p, H + 2 * p + 1)):
            rs[piece, pl.ds(groups * i + gg, no, stride=rows), :] = part

    loads[1].wait()

    def wait_halo(kind, j, n):
        for a, buf in enumerate((c0, solid)):
            part = buf.at[pl.ds(0, n)]
            pltpu.make_async_copy(part, part, halo_recv.at[kind, a, j]).wait()

    wait_halo(0, 0, H)

    def spread(c, q, w):
        b = F32(time_step * 0.25) - F32(time_step * 0.25 * solid_drop) * solid[at(q[0] + q[1]), w, :]
        return b * (3.0 - 1.0 / (1.0 + c * c))

    def state(l, q, w):
        return cs[l][q[1] % 2, w, :] if l else c0[at(q[0] + q[1]), w, :]

    def diff(l, q, w):
        return ds[l][q[1] % 2, w, :]

    def after(q, n):
        return (q[0], q[1] + n)

    def store(l, q, w, c):
        i = q[1] % 2
        d = spread(c, q, w)
        if l:
            cs[l][i, w, :] = c
        ds[l][i, w, :] = d
        c_next[l, i, w, :] = pltpu.roll(c, ny - 1, 1)
        d_next[l, i, w, :] = pltpu.roll(d, ny - 1, 1)

    chunks = [pl.ds(r, ROWS) for r in range(0, nx, ROWS)]

    def prepare(q):
        for w in chunks:
            store(0, q, w, c0[at(q[0] + q[1]), w, :])

    def start_level(l):
        q, b = (0, l), (0, l - 1)
        for w in chunks:
            fz[l - 1, w, :] = (diff(l - 1, b, w) + diff(l - 1, q, w)) * (
                state(l - 1, q, w) - state(l - 1, b, w)
            )

    def advance(l, q):
        i = q[1] % 2
        for w in chunks:
            here, dh = state(l - 1, q, w), diff(l - 1, q, w)
            ahead = (dh + diff(l - 1, after(q, 1), w)) * (state(l - 1, after(q, 1), w) - here)
            new = (here + inflow[l - 1, i, w, :]) + (
                (ahead - fz[l - 1, w, :]) - outflow[l - 1, i, w, :]
            )
            fz[l - 1, w, :] = ahead
            if l < STEPS:
                store(l, q, w, new)
            else:
                fine_ref[at(q[0] + q[1]) - H, w, :] = new

    lanes = lax.broadcasted_iota(jnp.int32, (nx, ny), 1)
    rows_in = lax.broadcasted_iota(jnp.int32, (nx, ny), 0)

    def in_plane(l, q):
        i, w = q[1] % 2, pl.ds(0, nx)
        here, dh = state(l, q, w), diff(l, q, w)
        side = (dh + d_next[l, i]) * (c_next[l, i] - here)
        side = jnp.where(lanes < ny - 1, side, F32(0.0))
        outflow[l, i] = pltpu.roll(side, 1, 1)
        flux = (dh + pltpu.roll(dh, nx - 1, 0)) * (pltpu.roll(here, nx - 1, 0) - here)
        flux = jnp.where(rows_in < nx - 1, flux, F32(0.0))
        inflow[l, i] = (flux - pltpu.roll(flux, 1, 0)) + side

    def front(k, levels):
        prepare(after(k, 1))
        for l in range(1, levels + 1):
            advance(l, after(k, 1 - l))
        in_plane(0, after(k, 1))
        for l in range(1, min(levels, STEPS - 1) + 1):
            in_plane(l, after(k, 1 - l))

    prepare((0, 0))
    prepare((0, 1))
    in_plane(0, (0, 1))
    for l in range(1, STEPS):
        start_level(l)
        for k in (2 * l - 1, 2 * l):
            front((0, k), l)
    start_level(STEPS)

    def body(m):
        @pl.when(m >= planes // 2 - H // 2)
        def _():
            j = 2 * m - (planes - H)
            wait_halo(1, j, 1)
            wait_halo(1, j + 1, 1)

        for k in range(2):
            front((2 * m, 2 * STEPS - 1 + k), STEPS)
        q = H + 2 * m
        lo = jnp.minimum(at(q), at(q + 1)) - H
        plane = lo // 2
        piece = plane // per
        i = lax.rem(plane, per)
        for gg, part in enumerate(restrict(fine_ref, lo, lo + 1)):
            jl[piece, pl.ds(groups * i + gg, no, stride=rows), :] = part

    later = jnp.where(t == 0, F32(0.0), F32(1.0))

    def own(o):
        return pl.ds(pl.multiple_of(o * rows, rows), rows)

    @pl.loop(0, NP)
    def _(n):
        pl.loop(n * per, (n + 1) * per)(body)
        piece = jnp.where(core == 1, n, NP - 1 - n)
        for o in range(no):
            w = own(o)
            jl[piece, w, :] = jl[piece, w, :] - later * gl[o, piece] * rs[piece, w, :]

        @pl.when(n == 0)
        def _():
            @pl.when(place < half - 1)
            def _():
                pl.semaphore_wait(ready, 2 * (half - 1 - place))

            to_owners(lambda o: gl.at[o], gb.at[t], g_send, g_recv.at[group])

        to_owners(lambda o: jl.at[piece, own(o)], jb.at[piece, t], j_send.at[n], j_recv.at[n, group])
        jb[piece, t] = jl[piece, own(t), :]

    def scan(n, gr):
        piece = jnp.where(core == 1, n, NP - 1 - n)
        wait_either(group == gr, jb.at[piece], GROUP, j_recv.at[n, gr])
        for m in range(gr * GROUP, (gr + 1) * GROUP):
            x = jb[piece, m]
            if m:
                x = gb[m, piece] * xb[piece, m - 1] + x
            xb[piece, m] = x
        for m in range(gr * GROUP, (gr + 1) * GROUP):
            @pl.when(t == m)
            def _(m=m):
                ob[piece, t] = xb[piece, m]

            @pl.when(t != m)
            def _(m=m):
                pltpu.make_async_remote_copy(
                    src_ref=xb.at[piece, m], dst_ref=ob.at[piece, t],
                    send_sem=x_send.at[n], recv_sem=x_recv.at[n],
                    device_id={"tm": m}, device_id_type=MESH,
                ).start()

    for grs in ((0,), (1, 2), (3,)):
        for gr in grs:
            wait_either(group == gr, gb, GROUP, g_recv.at[gr])

        @pl.loop(0, NP)
        def _(n):
            for gr in grs:
                scan(n, gr)

    for n in range(NP):
        wait_blocks(ob.at[0], no - 1, x_recv.at[n])
    for g in range(gv.shape[1] // 128):
        for piece in range(NP):
            coarse_ref[pl.ds(piece * per, per), pl.ds(g * 128, 128)] = ob[
                piece, g // groups, pl.ds(g % groups, per, stride=groups), :
            ]

    for cp in fast_copies:
        cp.wait_send()

    @pl.when(inner)
    def _():
        for cp in slow_copies:
            cp.wait_send()

    wait_blocks(gl, no - 1, g_send)
    for n in range(NP):
        wait_blocks(ob.at[0], no - 1, j_send.at[n])
        wait_blocks(xb.at[0], nt - 1, x_send.at[n])


def on_device(nt, ns, start_state, solid_fraction, coarse_gain):
    planes, nx, ny = solid_fraction.shape
    ext = planes + 2 * H
    cp, cells = coarse_gain.shape[1:]
    no = nt
    rows = cp * cells // 128 // no // NP
    vmem = lambda *shape: pltpu.VMEM(shape, F32)
    dma = pltpu.SemaphoreType.DMA
    fine, coarse = pl.pallas_call(
        functools.partial(kernel, nt, ns),
        name="parareal",
        out_shape=(
            pltpu.VMEM((planes, nx, ny), F32),
            pltpu.VMEM((cp, cells), F32),
        ),
        in_specs=[pl.BlockSpec(memory_space=pltpu.HBM)] * 3,
        out_specs=(pl.BlockSpec(memory_space=pltpu.VMEM), pl.BlockSpec(memory_space=pltpu.VMEM)),
        scratch_shapes=[
            *[vmem(ext, nx, ny)] * 2, *[vmem(2, nx, ny)] * 7, *[vmem(STEPS, 2, nx, ny)] * 4,
            vmem(STEPS, nx, ny), vmem(nx, ny), vmem(2 * ny, ny),
            vmem(cp, cells), vmem(no, NP, rows, 128), vmem(NP, no * rows, 128), vmem(NP, no * rows, 128),
            vmem(nt, NP, rows, 128), vmem(NP, nt, rows, 128), vmem(NP, nt, rows, 128), vmem(NP, no, rows, 128),
            dma((3,)), dma((2, 2, H)), dma((2, 2, H)), dma, dma((nt // GROUP,)),
            dma((NP,)), dma((NP, nt // GROUP)), dma((NP,)), dma((NP,)), pltpu.SemaphoreType.REGULAR,
        ],
        compiler_params=pltpu.CompilerParams(
            collective_id=0, has_side_effects=True, vmem_limit_bytes=46 * 2**20
        ),
    )(*[pltpu.with_memory_space_constraint(v, pltpu.HBM) for v in (start_state[0], solid_fraction, coarse_gain[0])])
    return fine[None], coarse[None]


def solution(mesh):
    nt, ns = mesh.shape["tm"], mesh.shape["space"]
    placed = (P("tm", "space", None, None), P("space", None, None), P("tm", "space", None))
    return jax.shard_map(
        functools.partial(on_device, nt, ns),
        mesh=mesh,
        in_specs=placed,
        out_specs=(P("tm", "space", None, None), P("tm", "space", None)),
        check_vma=False,
    )
```

```python
import functools

import jax
import jax.numpy as jnp
from jax import lax
from jax.experimental import pallas as pl
from jax.experimental.pallas import tpu as pltpu
from jax.sharding import PartitionSpec as P

STEPS = 4
H = STEPS
F32 = jnp.float32
MESH = pl.DeviceIdType.MESH

time_step = 0.11
solid_drop = 0.9

ROWS = 32
NP = 4
GROUP = 4


def kernel(
    nt, ns, c_hbm, s_hbm, g_hbm, fine_ref, coarse_ref,
    c0, solid, c1, c2, c3, d0, d1, d2, d3, c_next, d_next, inflow, outflow, fz, vs, ly,
    gv, gl, rs, jl, gb, jb, xb, ob,
    ld_sem, halo_send, halo_recv, g_send, g_recv, j_send, j_recv, x_send, x_recv, ready,
):
    planes, nx, ny = c_hbm.shape
    cs = (c0, c1, c2, c3)
    ds = (d0, d1, d2, d3)
    half = nt // 2
    no = nt
    t = lax.axis_index("tm")
    s = lax.axis_index("space")
    core = lax.rem(s, 2)
    step = 2 * core - 1
    first = jnp.where(core == 1, 0, planes + 2 * H - 1)

    def at(q):
        return first + step * q

    place = lax.rem(t, half)
    group = t // GROUP
    partners = [lax.rem(t + k, nt) for k in range(1, nt)]

    barrier = pltpu.get_barrier_semaphore()
    for q in partners:
        @pl.when(lax.rem(q, half) >= place)
        def _(q=q):
            pl.semaphore_signal(barrier, inc=1, device_id={"tm": q}, device_id_type=MESH)

    fast = s + 1 - 2 * core
    slow = s - 1 + 2 * core
    inner = jnp.logical_and(slow >= 0, slow < ns)
    pl.semaphore_signal(barrier, inc=1, device_id={"space": fast}, device_id_type=MESH)

    other = lax.rem(t + half, nt)

    @pl.when(inner)
    def _():
        for to in (t, other):
            pl.semaphore_signal(barrier, inc=1, device_id={"tm": to, "space": slow}, device_id_type=MESH)

    loads = [
        pltpu.make_async_copy(c_hbm, c0.at[pl.ds(H, planes)], ld_sem.at[0]),
        pltpu.make_async_copy(s_hbm, solid.at[pl.ds(H, planes)], ld_sem.at[1]),
        pltpu.make_async_copy(g_hbm, gv, ld_sem.at[2]),
    ]
    for cp in loads:
        cp.start()

    def sends(to_high, dev, kind, n, solid_to):
        out = []
        for j in range(H // n):
            src = jnp.where(to_high, planes - n * (j + 1), n * j)
            dst = jnp.where(to_high, H - n * (j + 1), H + planes + n * j)
            for a, (ref, buf) in enumerate(((c_hbm, c0), (s_hbm, solid))):
                to = buf.at[pl.ds(dst, n)]
                out.append(
                    pltpu.make_async_remote_copy(
                        src_ref=ref.at[pl.ds(src, n)], dst_ref=to,
                        send_sem=halo_send.at[kind, a, j], recv_sem=halo_recv.at[kind, a, j],
                        device_id={"tm": (t, solid_to)[a], "space": dev}, device_id_type=MESH,
                    )
                )
        return out

    fast_copies = sends(core == 0, fast, 0, H, t)
    slow_copies = sends(core == 1, slow, 1, 1, other)

    def mirrors():
        out = []
        for j in range(H):
            src = jnp.where(core == 1, planes - 1 - j, j)
            dst = jnp.where(core == 1, H + planes + j, H - 1 - j)
            for a, (ref, buf) in enumerate(((c_hbm, c0), (s_hbm, solid))):
                out.append(
                    pltpu.make_async_copy(ref.at[src], buf.at[dst], halo_recv.at[1, a, j])
                )
        return out

    pl.semaphore_wait(barrier, 2 * place + 2 + jnp.where(inner, 2, 0))

    @pl.when(inner)
    def _():
        for cp in slow_copies:
            cp.start()

    @pl.when(jnp.logical_not(inner))
    def _():
        for cp in mirrors():
            cp.start()

    for cp in fast_copies:
        cp.start()

    for q in partners:
        @pl.when(lax.rem(q, half) < place)
        def _(q=q):
            pl.semaphore_signal(ready, inc=1, device_id={"tm": q}, device_id_type=MESH)

    row = lax.broadcasted_iota(jnp.int32, (2 * ny, ny), 0)
    lane = lax.broadcasted_iota(jnp.int32, (2 * ny, ny), 1)
    ly[...] = jnp.where(row // 2 == lane, F32(0.125), F32(0.0))

    per = planes // 2 // NP
    groups = 32 // no
    rows = groups * per

    def restrict(ref, lo, hi):
        vs[...] = ref[lo] + ref[hi]
        parts = []
        for gg in range(groups):
            halves = []
            for h in range(2):
                base = 4 * gg + 2 * h
                halves.append(
                    vs[pl.ds(base, no, stride=nx // no), :] + vs[pl.ds(base + 1, no, stride=nx // no), :]
                )
            parts.append(jnp.concatenate(halves, axis=1))
        both = jnp.concatenate(parts, axis=0)
        out = jnp.dot(both, ly[...], precision=lax.Precision.HIGHEST, preferred_element_type=F32)
        return [out[no * gg : no * (gg + 1)] for gg in range(groups)]

    loads[2].wait()
    for g in range(gv.shape[1] // 128):
        v = gv[:, pl.ds(g * 128, 128)]
        for piece in range(NP):
            gl[g // groups, piece, pl.ds(g % groups, per, stride=groups), :] = v[
                piece * per : (piece + 1) * per
            ]

    def to_owners(src, dst, send, recv):
        for q in partners:
            pltpu.make_async_remote_copy(
                src_ref=src(q), dst_ref=dst, send_sem=send, recv_sem=recv,
                device_id={"tm": q}, device_id_type=MESH,
            ).start()

    def wait_blocks(ref, n, sem):
        part = ref.at[pl.ds(0, n)]
        pltpu.make_async_copy(part, part, sem).wait()

    def wait_either(cond, ref, n, sem):
        @pl.when(cond)
        def _():
            wait_blocks(ref, n - 1, sem)

        @pl.when(jnp.logical_not(cond))
        def _():
            wait_blocks(ref, n, sem)

    gb[t] = gl[t]

    loads[0].wait()

    @pl.loop(0, planes // 2)
    def _(p):
        piece = p // per
        i = lax.rem(p, per)
        for gg, part in enumerate(restrict(c0, H + 2 * p, H + 2 * p + 1)):
            rs[piece, pl.ds(groups * i + gg, no, stride=rows), :] = part

    loads[1].wait()

    def wait_halo(kind, j, n):
        for a, buf in enumerate((c0, solid)):
            part = buf.at[pl.ds(0, n)]
            pltpu.make_async_copy(part, part, halo_recv.at[kind, a, j]).wait()

    wait_halo(0, 0, H)

    def spread(c, q, w):
        b = F32(time_step * 0.25) - F32(time_step * 0.25 * solid_drop) * solid[at(q[0] + q[1]), w, :]
        return b * (3.0 - 1.0 / (1.0 + c * c))

    def state(l, q, w):
        return cs[l][q[1] % 2, w, :] if l else c0[at(q[0] + q[1]), w, :]

    def diff(l, q, w):
        return ds[l][q[1] % 2, w, :]

    def after(q, n):
        return (q[0], q[1] + n)

    def store(l, q, w, c):
        i = q[1] % 2
        d = spread(c, q, w)
        if l:
            cs[l][i, w, :] = c
        ds[l][i, w, :] = d
        c_next[l, i, w, :] = pltpu.roll(c, ny - 1, 1)
        d_next[l, i, w, :] = pltpu.roll(d, ny - 1, 1)

    chunks = [pl.ds(r, ROWS) for r in range(0, nx, ROWS)]

    def prepare(q):
        for w in chunks:
            store(0, q, w, c0[at(q[0] + q[1]), w, :])

    def start_level(l):
        q, b = (0, l), (0, l - 1)
        for w in chunks:
            fz[l - 1, w, :] = (diff(l - 1, b, w) + diff(l - 1, q, w)) * (
                state(l - 1, q, w) - state(l - 1, b, w)
            )

    def advance(l, q):
        i = q[1] % 2
        for w in chunks:
            here, dh = state(l - 1, q, w), diff(l - 1, q, w)
            ahead = (dh + diff(l - 1, after(q, 1), w)) * (state(l - 1, after(q, 1), w) - here)
            new = (here + inflow[l - 1, i, w, :]) + (
                (ahead - fz[l - 1, w, :]) - outflow[l - 1, i, w, :]
            )
            fz[l - 1, w, :] = ahead
            if l < STEPS:
                store(l, q, w, new)
            else:
                fine_ref[at(q[0] + q[1]) - H, w, :] = new

    lanes = lax.broadcasted_iota(jnp.int32, (nx, ny), 1)
    rows_in = lax.broadcasted_iota(jnp.int32, (nx, ny), 0)

    def in_plane(l, q):
        i, w = q[1] % 2, pl.ds(0, nx)
        here, dh = state(l, q, w), diff(l, q, w)
        side = (dh + d_next[l, i]) * (c_next[l, i] - here)
        side = jnp.where(lanes < ny - 1, side, F32(0.0))
        outflow[l, i] = pltpu.roll(side, 1, 1)
        flux = (dh + pltpu.roll(dh, nx - 1, 0)) * (pltpu.roll(here, nx - 1, 0) - here)
        flux = jnp.where(rows_in < nx - 1, flux, F32(0.0))
        inflow[l, i] = (flux - pltpu.roll(flux, 1, 0)) + side

    def front(k, levels):
        prepare(after(k, 1))
        for l in range(1, levels + 1):
            advance(l, after(k, 1 - l))
        in_plane(0, after(k, 1))
        for l in range(1, min(levels, STEPS - 1) + 1):
            in_plane(l, after(k, 1 - l))

    prepare((0, 0))
    prepare((0, 1))
    in_plane(0, (0, 1))
    for l in range(1, STEPS):
        start_level(l)
        for k in (2 * l - 1, 2 * l):
            front((0, k), l)
    start_level(STEPS)

    def body(m):
        @pl.when(m >= planes // 2 - H // 2)
        def _():
            j = 2 * m - (planes - H)
            wait_halo(1, j, 1)
            wait_halo(1, j + 1, 1)

        for k in range(2):
            front((2 * m, 2 * STEPS - 1 + k), STEPS)
        q = H + 2 * m
        lo = jnp.minimum(at(q), at(q + 1)) - H
        plane = lo // 2
        piece = plane // per
        i = lax.rem(plane, per)
        for gg, part in enumerate(restrict(fine_ref, lo, lo + 1)):
            jl[piece, pl.ds(groups * i + gg, no, stride=rows), :] = part

    later = jnp.where(t == 0, F32(0.0), F32(1.0))

    def own(o):
        return pl.ds(pl.multiple_of(o * rows, rows), rows)

    @pl.loop(0, NP)
    def _(n):
        pl.loop(n * per, (n + 1) * per)(body)
        piece = jnp.where(core == 1, n, NP - 1 - n)
        for o in range(no):
            w = own(o)
            jl[piece, w, :] = jl[piece, w, :] - later * gl[o, piece] * rs[piece, w, :]

        @pl.when(n == 0)
        def _():
            @pl.when(place < half - 1)
            def _():
                pl.semaphore_wait(ready, 2 * (half - 1 - place))

            to_owners(lambda o: gl.at[o], gb.at[t], g_send, g_recv.at[group])

        to_owners(lambda o: jl.at[piece, own(o)], jb.at[piece, t], j_send.at[n], j_recv.at[n, group])
        jb[piece, t] = jl[piece, own(t), :]

    def scan(n, gr):
        piece = jnp.where(core == 1, n, NP - 1 - n)
        wait_either(group == gr, jb.at[piece], GROUP, j_recv.at[n, gr])
        for m in range(gr * GROUP, (gr + 1) * GROUP):
            if m == 0:
                x = jb[piece, m]
            elif m == gr * GROUP:
                x = gb[m, piece] * xb[piece, m - 1] + jb[piece, m]
            else:
                x = gb[m, piece] * x + jb[piece, m]
            xb[piece, m] = x
        for m in range(gr * GROUP, (gr + 1) * GROUP):
            @pl.when(t == m)
            def _(m=m):
                ob[piece, t] = xb[piece, m]

            @pl.when(t != m)
            def _(m=m):
                pltpu.make_async_remote_copy(
                    src_ref=xb.at[piece, m], dst_ref=ob.at[piece, t],
                    send_sem=x_send.at[n], recv_sem=x_recv.at[n],
                    device_id={"tm": m}, device_id_type=MESH,
                ).start()

    for grs in ((0,), (1, 2), (3,)):
        for gr in grs:
            wait_either(group == gr, gb, GROUP, g_recv.at[gr])

        @pl.loop(0, NP)
        def _(n):
            for gr in grs:
                scan(n, gr)

    for n in range(NP):
        wait_blocks(ob.at[0], no - 1, x_recv.at[n])
        for at_piece, here in ((n, core == 1), (NP - 1 - n, core == 0)):
            @pl.when(here)
            def _(piece=at_piece):
                for g in range(gv.shape[1] // 128):
                    coarse_ref[pl.ds(piece * per, per), pl.ds(g * 128, 128)] = ob[
                        piece, g // groups, pl.ds(g % groups, per, stride=groups), :
                    ]

    for cp in fast_copies:
        cp.wait_send()

    @pl.when(inner)
    def _():
        for cp in slow_copies:
            cp.wait_send()

    wait_blocks(gl, no - 1, g_send)
    for n in range(NP):
        wait_blocks(ob.at[0], no - 1, j_send.at[n])
        wait_blocks(xb.at[0], nt - 1, x_send.at[n])


def on_device(nt, ns, start_state, solid_fraction, coarse_gain):
    planes, nx, ny = solid_fraction.shape
    ext = planes + 2 * H
    cp, cells = coarse_gain.shape[1:]
    no = nt
    rows = cp * cells // 128 // no // NP
    vmem = lambda *shape: pltpu.VMEM(shape, F32)
    dma = pltpu.SemaphoreType.DMA
    fine, coarse = pl.pallas_call(
        functools.partial(kernel, nt, ns),
        name="parareal",
        out_shape=(
            pltpu.VMEM((planes, nx, ny), F32),
            pltpu.VMEM((cp, cells), F32),
        ),
        in_specs=[pl.BlockSpec(memory_space=pltpu.HBM)] * 3,
        out_specs=(pl.BlockSpec(memory_space=pltpu.VMEM), pl.BlockSpec(memory_space=pltpu.VMEM)),
        scratch_shapes=[
            *[vmem(ext, nx, ny)] * 2, *[vmem(2, nx, ny)] * 7, *[vmem(STEPS, 2, nx, ny)] * 4,
            vmem(STEPS, nx, ny), vmem(nx, ny), vmem(2 * ny, ny),
            vmem(cp, cells), vmem(no, NP, rows, 128), vmem(NP, no * rows, 128), vmem(NP, no * rows, 128),
            vmem(nt, NP, rows, 128), vmem(NP, nt, rows, 128), vmem(NP, nt, rows, 128), vmem(NP, no, rows, 128),
            dma((3,)), dma((2, 2, H)), dma((2, 2, H)), dma, dma((nt // GROUP,)),
            dma((NP,)), dma((NP, nt // GROUP)), dma((NP,)), dma((NP,)), pltpu.SemaphoreType.REGULAR,
        ],
        compiler_params=pltpu.CompilerParams(
            collective_id=0, has_side_effects=True, vmem_limit_bytes=46 * 2**20
        ),
    )(*[pltpu.with_memory_space_constraint(v, pltpu.HBM) for v in (start_state[0], solid_fraction, coarse_gain[0])])
    return fine[None], coarse[None]


def solution(mesh):
    nt, ns = mesh.shape["tm"], mesh.shape["space"]
    placed = (P("tm", "space", None, None), P("space", None, None), P("tm", "space", None))
    return jax.shard_map(
        functools.partial(on_device, nt, ns),
        mesh=mesh,
        in_specs=placed,
        out_specs=(P("tm", "space", None, None), P("tm", "space", None)),
        check_vma=False,
    )
```
